256 devices in a mesh: layer: 8 (over x, core), space: 32 (over y, z).
Axes of the slice: x: 4, y: 4, z: 8, core: 2. Of those that a mesh axis runs over, the one named last changes fastest.
Arguments:
- initial: float32 [8, 128, 16, 128], P(None, 'space'), may hold values from -6 to 6
- guess: float32 [8, 8, 128, 16, 128], P('layer', None, 'space'), may hold values from -6 to 6
- weights: float32 [32, 8, 216], P('layer'), may hold values from -0.4375 to 0.4375
- bias: float32 [32, 8], P('layer'), may hold values from -3 to 3
Outputs:
- corrected: float32 [8, 8, 128, 16, 128], P('layer', None, 'space')
- residual: float32 [8, 8, 128, 16, 128], P('layer', None, 'space')
The draws below stay inside these ranges and needn't reach their ends.
All inputs are finite; a program needn't handle non-finite values.
Results may differ from the reference program's by a relative error of at most 0.00011.
Values sent between devices are 32-bit elements; how exact they have to be, the bound alone decides.
No kernel may reach another device: no remote copies, remote signals or barrier semaphores. Data moves between devices by JAX's collectives and lax.ppermute only.
A program may use at most 128 MiB of HBM per device.

```python
import jax
import jax.numpy as jnp
from jax import lax

C = 8
GROUP = 4
NX = 16
NY = 128
COARSE = 8
STEPS = 32
NZ = 128


def block_scale(rng, extent, cuts, least, top_value):
    def one(axis_at, shards_of):
        draws = jax.random.uniform(jax.random.fold_in(jax.random.fold_in(rng, 6), axis_at), (shards_of,), jnp.float32, least / len(cuts), top_value / len(cuts))
        return jnp.repeat(jnp.exp(draws), extent[axis_at] // shards_of).reshape((-1,) + (1,) * (len(extent) - axis_at - 1))

    loudness = one(*cuts[0])
    for cut in cuts[1:]:
        loudness = loudness * one(*cut)
    return loudness


def centred(rng, dims, deviation, reach, cuts=(), held_as=jnp.bfloat16):
    drawn = deviation * jax.random.normal(rng, dims, jnp.float32)
    if cuts:
        drawn = drawn * block_scale(rng, dims, cuts, -0.22, 0.18)
    return jnp.clip(drawn, -reach, reach).astype(held_as)


def setup_inputs(seed: int = 0) -> dict:
    seeds = jax.random.split(jax.random.key(seed), 5)
    initial = centred(seeds[0], (C, NZ, NX, NY), 1.0, 6.0, ((1, 32),), jnp.float32)
    guess = centred(seeds[1], (COARSE, C, NZ, NX, NY), 1.0, 6.0, ((0, 8), (2, 32)), jnp.float32)
    weights = centred(seeds[2], (STEPS, C, 27 * C), (27 * C) ** -0.5, 0.4375, ((0, 8),), jnp.float32)
    bias = centred(seeds[3], (STEPS, C), 0.5, 3.0, ((0, 8),), jnp.float32)
    return dict(initial=initial, guess=guess, weights=weights, bias=bias)


fine_step = 0.25
coarse_step = 1.0


def layer_update(state, padded, kernel, offset, step):
    channels, depth, rows, width = state.shape
    pieces = [padded[:, a:a + depth, b:b + rows, c:c + width] for a in range(3) for b in range(3) for c in range(3)]
    columns = jnp.concatenate(pieces, 0).reshape(27 * channels, -1)
    mixed = jnp.dot(kernel, columns, precision=lax.Precision.HIGHEST, preferred_element_type=jnp.float32)
    mixed = mixed.reshape(state.shape)
    return state + step * jnp.tanh(mixed + offset[:, None, None, None])


def padded_all(state):
    return jnp.pad(state, ((0, 0), (1, 1), (1, 1), (1, 1)))


def block_run(state, weights, bias, first):
    for inner in range(GROUP):
        state = layer_update(state, padded_all(state), weights[first + inner], bias[first + inner], fine_step)
    return state


def coarse_update(state, weights, bias, first):
    return layer_update(state, padded_all(state), weights[first], bias[first], coarse_step)


def reference(initial, guess, weights, bias):
    blocks = guess.shape[0]
    relaxed = []
    for block in range(blocks):
        start = initial if block == 0 else guess[block - 1]
        relaxed.append(block_run(start, weights, bias, GROUP * block))
    residual = []
    forcing = []
    for block in range(blocks):
        begin = initial if block == 0 else relaxed[block - 1]
        propagated = block_run(begin, weights, bias, GROUP * block)
        residual.append(propagated - relaxed[block])
        forcing.append(propagated - coarse_update(begin, weights, bias, GROUP * block))
    corrected = []
    coarse_state = initial
    for block in range(blocks):
        coarse_state = coarse_update(coarse_state, weights, bias, GROUP * block) + forcing[block]
        corrected.append(coarse_state)
    return jnp.stack(corrected), jnp.stack(residual)
```

```python
import functools

import jax
import jax.numpy as jnp
from jax import lax
from jax.experimental import pallas as pl
from jax.experimental.pallas import tpu as pltpu
from jax.sharding import PartitionSpec as P

FINE = 0.25
COARSE = 1.0
LANES = 128
ROWS = 128
TAPS = 3
BAND = TAPS * ROWS
SLAB = 4
VMEM_LIMIT = 40 * 1024 * 1024


def split(value):
    high = value.astype(jnp.bfloat16)
    low = (value - high.astype(jnp.float32)).astype(jnp.bfloat16)
    return high, low


def band_kernel(taps_ref, high_ref, low_ref):
    channel = 16
    row = lax.broadcasted_iota(jnp.int32, (channel, BAND), 0)
    column = lax.broadcasted_iota(jnp.int32, (channel, BAND), 1) % channel
    masks = [column - row == tap - 1 for tap in range(TAPS)]
    for block in range(BAND // channel):
        total = jnp.zeros((channel, BAND), jnp.float32)
        for tap in range(TAPS):
            total = total + jnp.where(masks[tap], taps_ref[0, tap, block : block + 1, :], 0.0)
        high, low = split(total)
        high_ref[0, block * channel : (block + 1) * channel, :] = high
        low_ref[0, block * channel : (block + 1) * channel, :] = low


def band_matrices(taps):
    count = taps.shape[0]
    matrix = pl.BlockSpec((1, BAND, BAND), lambda n: (n, 0, 0))
    shape = jax.ShapeDtypeStruct((count, BAND, BAND), jnp.bfloat16)
    return pl.pallas_call(
        band_kernel,
        grid=(count,),
        in_specs=[pl.BlockSpec((1,) + taps.shape[1:], lambda n: (n, 0, 0, 0))],
        out_specs=[matrix, matrix],
        out_shape=[shape, shape],
        cost_estimate=pl.CostEstimate(flops=count * 2000000, bytes_accessed=count * 700000, transcendentals=0),
    )(taps)


def window(planes, at, count):
    pieces = [planes[(p - 1) * ROWS : (p + 2) * ROWS, :] for p in range(at, at + count)]
    return pieces[0] if count == 1 else jnp.concatenate(pieces, axis=1)


def activations(high, low, wide, narrow, bias, at, count):
    right = window(high, at, count)
    mixed = jnp.dot(wide, right, preferred_element_type=jnp.float32)
    mixed += jnp.dot(narrow, right, preferred_element_type=jnp.float32)
    mixed += jnp.dot(wide, window(low, at, count), preferred_element_type=jnp.float32)
    lane = lax.broadcasted_iota(jnp.int32, (ROWS, LANES), 1)
    results = []
    for j in range(count):
        part = mixed[:, j * LANES : (j + 1) * LANES]
        before = pltpu.roll(part[:ROWS], 1, axis=1)
        after = pltpu.roll(part[2 * ROWS :], LANES - 1, axis=1)
        conv = part[ROWS : 2 * ROWS] + bias
        conv = conv + jnp.where(lane == 0, 0.0, before) + jnp.where(lane == LANES - 1, 0.0, after)
        results.append(jnp.tanh(conv))
    return results


def store_split(high, low, slot, plane, value):
    h, l = split(value)
    high[slot, plane * ROWS : (plane + 1) * ROWS, :] = h
    low[slot, plane * ROWS : (plane + 1) * ROWS, :] = l


def block_kernel(by_channel, forcing, flags, left, middle, right, wide, narrow, bias, *refs):
    if forcing:
        out, minus, state, high, low, coarse = refs
    else:
        out, state, high, low = refs
    steps = wide.shape[0]
    planes = 3 * SLAB
    scale = {0: flags[0].astype(jnp.float32), 2: flags[1].astype(jnp.float32)}

    def inside(plane, value):
        side = plane // SLAB
        return value * scale[side] if side != 1 else value

    for plane in range(planes):
        source = (left, middle, right)[plane // SLAB]
        value = source[:, plane % SLAB].reshape(ROWS, LANES) if by_channel else source[plane % SLAB]
        value = inside(plane, value)
        state[plane] = value
        store_split(high, low, 0, plane, value)
    for step in range(steps):
        first, last = step + 1, planes - 1 - step
        now, later = step % 2, (step + 1) % 2
        for at in range(first, last, 2):
            outs = activations(high.at[now], low.at[now], wide[step], narrow[step], bias[step], at, 2)
            for plane, change in zip((at, at + 1), outs):
                old = state[plane]
                value = inside(plane, old + FINE * change)
                own = SLAB <= plane < 2 * SLAB
                if forcing and step == 0 and own:
                    coarse[plane - SLAB] = old + COARSE * change
                if step < steps - 1:
                    state[plane] = value
                    store_split(high, low, later, plane, value)
                else:
                    out[plane - SLAB] = value
                    if forcing:
                        keep = flags[2].astype(jnp.float32)
                        minus[plane - SLAB] = value - coarse[plane - SLAB] * keep


VMEM = pl.BlockSpec(memory_space=pltpu.VMEM)
SMEM = pl.BlockSpec(memory_space=pltpu.SMEM)


def run_block(flags, left, middle, right, wide, narrow, bias, by_channel, forcing):
    planes = 3 * SLAB
    shape = jax.ShapeDtypeStruct((SLAB, ROWS, LANES), jnp.float32)
    scratch = [
        pltpu.VMEM((planes, ROWS, LANES), jnp.float32),
        pltpu.VMEM((2, planes * ROWS, LANES), jnp.bfloat16),
        pltpu.VMEM((2, planes * ROWS, LANES), jnp.bfloat16),
    ]
    if forcing:
        scratch.append(pltpu.VMEM((SLAB, ROWS, LANES), jnp.float32))
    return pl.pallas_call(
        functools.partial(block_kernel, by_channel, forcing),
        in_specs=[SMEM] + [VMEM] * 6,
        out_specs=[VMEM] * (2 if forcing else 1),
        out_shape=[shape] * (2 if forcing else 1),
        scratch_shapes=scratch,
        compiler_params=pltpu.CompilerParams(vmem_limit_bytes=VMEM_LIMIT),
        cost_estimate=pl.CostEstimate(flops=4000000000, bytes_accessed=6000000, transcendentals=500000),
    )(flags, left, middle, right, wide, narrow, bias)


def sweep_kernel(flags, mine, near, far, own, swapped, edge, wide, narrow, bias, first_out, second_out, state, high, low):
    lower = flags[0] == 0
    left_scale, right_scale = flags[1].astype(jnp.float32), flags[2].astype(jnp.float32)

    def pick(a, b):
        return jnp.where(lower, a, b)

    for j in range(2):
        values = {
            j: pick(far[j], near[j]) * left_scale,
            2 + j: mine[j],
            4 + j: pick(near[j], far[j]) * right_scale,
        }
        for plane, value in values.items():
            state[plane] = value
            store_split(high, low, 0, plane, value)
    forcing = {
        1: lambda: pick(edge[0], swapped[1]),
        2: lambda: pick(own[0], swapped[2]),
        3: lambda: pick(own[1], swapped[3]),
        4: lambda: pick(own[2], edge[0]),
    }
    for at in (1, 3):
        outs = activations(high.at[0], low.at[0], wide[0], narrow[0], bias[0], at, 2)
        for plane, change in zip((at, at + 1), outs):
            value = state[plane] + COARSE * change + forcing[plane]()
            if plane == 1:
                value = value * left_scale
            if plane == 4:
                value = value * right_scale
            state[plane] = value
            store_split(high, low, 1, plane, value)
            if plane in (2, 3):
                first_out[plane - 2] = value
    outs = activations(high.at[1], low.at[1], wide[1], narrow[1], bias[1], 2, 2)
    for j, change in enumerate(outs):
        second_out[j] = state[2 + j] + COARSE * change + pick(swapped[j], own[2 + j])


def run_sweep(flags, mine, near, far, own, swapped, edge, wide, narrow, bias):
    shape = jax.ShapeDtypeStruct((2, ROWS, LANES), jnp.float32)
    return pl.pallas_call(
        sweep_kernel,
        in_specs=[SMEM] + [VMEM] * 9,
        out_specs=[VMEM] * 2,
        out_shape=[shape] * 2,
        scratch_shapes=[
            pltpu.VMEM((6, ROWS, LANES), jnp.float32),
            pltpu.VMEM((2, 6 * ROWS, LANES), jnp.bfloat16),
            pltpu.VMEM((2, 6 * ROWS, LANES), jnp.bfloat16),
        ],
        compiler_params=pltpu.CompilerParams(vmem_limit_bytes=VMEM_LIMIT),
        cost_estimate=pl.CostEstimate(flops=900000000, bytes_accessed=4000000, transcendentals=100000),
    )(flags, mine, near, far, own, swapped, edge, wide, narrow, bias)


def on_device(layers, slabs, initial, guess, weights, bias):
    layer = lax.axis_index("layer")
    slab = lax.axis_index("space")
    core = layer % 2
    lower = core == 0

    def send(array, target):
        pairs = []
        for l in range(layers):
            for s in range(slabs):
                to_l, to_s = target(l, s)
                pairs.append((l * slabs + s, (to_l % layers) * slabs + to_s % slabs))
        return lax.ppermute(array, ("layer", "space"), pairs)

    def up(l, s):
        return l, s + 1

    def down(l, s):
        return l, s - 1

    def across(l, s):
        return l ^ 1, s

    def zigzag(l, s):
        return (l + 1, s - 1) if l % 2 == 0 else (l - 1, s + 1)

    def shifted(by, then=lambda l, s: (l, s)):
        def target(l, s):
            l, s = then(l, s)
            return l + by, s

        return target

    not_first = (slab > 0).astype(jnp.int32)
    not_last = (slab < slabs - 1).astype(jnp.int32)

    start = jnp.where(layer == layers - 1, initial, guess[0])
    below, above = send(start, up), send(start, down)

    packed = lax.all_gather(jnp.concatenate([weights, bias[:, :, None]], 2), "layer", tiled=True)
    group = weights.shape[0]
    pieces = [
        lax.dynamic_slice_in_dim(packed, group * ((layer + 1) % layers), group),
        lax.dynamic_slice_in_dim(packed, group * ((layer + 2) % layers), group),
        packed[2 * group :: group],
    ]

    def prepare(piece):
        count, channels, _ = piece.shape
        kernel = piece[:, :, :-1].reshape(count, channels, TAPS, TAPS, TAPS, channels)
        kernel = kernel.transpose(0, 3, 4, 1, 2, 5).reshape(count, TAPS, TAPS * channels, TAPS * channels)
        wide, narrow = band_matrices(jnp.repeat(kernel, ROWS // channels, axis=3))
        offset = jnp.repeat(piece[:, :, -1], ROWS // channels, axis=1)
        return wide, narrow, jnp.broadcast_to(offset[:, :, None], (count, ROWS, LANES))

    first, second, sweep = [prepare(piece) for piece in pieces]
    edges = jnp.stack([not_first, not_last, (layer < layers - 1).astype(jnp.int32)])
    (relaxed,) = run_block(edges, below, start, above, *first, by_channel=True, forcing=False)

    below, above = send(relaxed, up), send(relaxed, down)
    relaxed_home = send(relaxed, shifted(1))
    propagated, forced = run_block(edges, below, relaxed, above, *second, by_channel=False, forcing=True)

    swapped = send(forced, across)
    even = jnp.where(lower, forced, swapped)
    odd = jnp.where(lower, swapped, forced)
    mine = jnp.where(lower, odd[:2], odd[2:])
    near = jnp.where(lower, odd[2:], odd[:2])
    rim = jnp.where(lower, even[:1], even[3:])
    met = send(jnp.concatenate([mine, rim], 0), zigzag)
    far, edge = met[:2], met[2:]
    flags = jnp.stack([core, jnp.where(lower, not_first, 1), jnp.where(lower, 1, not_last)]).astype(jnp.int32)

    terms = []
    r = send(forced, shifted(-2))
    terms.append((r, send(r, across), send(rim, shifted(-2, zigzag))))
    r = send(jnp.concatenate([forced, edge], 0), shifted(4))
    terms.append((r[:SLAB], send(r[:SLAB], across), r[SLAB:]))
    r = send(jnp.concatenate([forced, edge, propagated], 0), shifted(2))
    terms.append((r[:SLAB], send(r[:SLAB], across), r[SLAB : SLAB + 1]))
    propagated_home = r[SLAB + 1 :]

    ends = []
    for turn, (own, other, rim_in) in enumerate(terms):
        weights_now = [part[2 * turn : 2 * turn + 2] for part in sweep]
        a, b = run_sweep(flags, mine, near, far, own, other, rim_in, *weights_now)
        ends.append(jnp.concatenate([a, b], 0))
        if turn < 2:
            mine, near, far = b, send(b, across), send(b, zigzag)

    pair = jnp.where(
        layer // 2 == 1,
        send(ends[0], shifted(4)),
        jnp.where(layer // 2 == 2, send(ends[1], shifted(-2)), ends[2]),
    )
    kept = jnp.where(lower, pair[:2], pair[2:])
    got = send(jnp.where(lower, pair[2:], pair[:2]), across)
    corrected = jnp.where(lower, jnp.concatenate([kept, got], 0), jnp.concatenate([got, kept], 0))
    corrected = jnp.where(layer == 0, relaxed_home, jnp.where(layer == 1, propagated_home, corrected))
    residual = jnp.where(layer == 0, 0.0, propagated_home - relaxed_home)

    def by_channel(array):
        return array.reshape((SLAB,) + (initial.shape[0],) + initial.shape[2:]).transpose(1, 0, 2, 3)[None]

    return by_channel(corrected), by_channel(residual)


def solution(mesh):
    layers, slabs = mesh.shape["layer"], mesh.shape["space"]
    in_specs = (
        P(None, "space", None, None),
        P("layer", None, "space", None, None),
        P("layer", None, None),
        P("layer", None),
    )
    out_specs = (P("layer", None, "space", None, None), P("layer", None, "space", None, None))
    return jax.shard_map(
        functools.partial(on_device, layers, slabs),
        mesh=mesh,
        in_specs=in_specs,
        out_specs=out_specs,
        check_vma=False,
    )
```

```python
import functools

import jax
import jax.numpy as jnp
from jax import lax
from jax.experimental import pallas as pl
from jax.experimental.pallas import tpu as pltpu
from jax.sharding import PartitionSpec as P

FINE = 0.25
COARSE = 1.0
LANES = 128
ROWS = 128
TAPS = 3
BAND = TAPS * ROWS
SLAB = 4
CELLS = 16
KERNEL_ROWS = 72
PACKED_ROWS = 80
BIAS_AT = 256
VMEM_LIMIT = 40 * 1024 * 1024


def split(value):
    high = value.astype(jnp.bfloat16)
    low = (value - high.astype(jnp.float32)).astype(jnp.bfloat16)
    return high, low


def build_band(packed, wide, narrow, taps):
    lane = lax.broadcasted_iota(jnp.int32, (LANES, BAND), 1)
    spread = jnp.where(lane // CELLS == lax.broadcasted_iota(jnp.int32, (LANES, BAND), 0), 1.0, 0.0)
    high, low = split(packed[:KERNEL_ROWS, :])
    both = jnp.concatenate([high, low], axis=0)
    taps[...] = jnp.dot(both, spread.astype(jnp.bfloat16), preferred_element_type=jnp.float32)
    row = lax.broadcasted_iota(jnp.int32, (CELLS, BAND), 0)
    offset = lax.broadcasted_iota(jnp.int32, (CELLS, BAND), 1) % CELLS - row
    blocks = BAND // CELLS
    for part, target in enumerate((wide, narrow)):
        for block in range(blocks):
            total = jnp.zeros((CELLS, BAND), jnp.float32)
            for tap in range(TAPS):
                at = part * KERNEL_ROWS + tap * blocks + block
                total = jnp.where(offset == tap - 1, taps[at : at + 1, :], total)
            target[block * CELLS : (block + 1) * CELLS, :] = total.astype(jnp.bfloat16)


def offsets(packed):
    rows = [jnp.broadcast_to(packed[at : at + 1, :], (CELLS, LANES)) for at in range(KERNEL_ROWS, PACKED_ROWS)]
    return jnp.concatenate(rows, axis=0)


def window(planes, at, count):
    pieces = [planes[(p - 1) * ROWS : (p + 2) * ROWS, :] for p in range(at, at + count)]
    return pieces[0] if count == 1 else jnp.concatenate(pieces, axis=1)


def activations(high, low, wide, narrow, bias, at, count):
    right = window(high, at, count)
    mixed = jnp.dot(wide, right, preferred_element_type=jnp.float32)
    mixed += jnp.dot(narrow, right, preferred_element_type=jnp.float32)
    mixed += jnp.dot(wide, window(low, at, count), preferred_element_type=jnp.float32)
    lane = lax.broadcasted_iota(jnp.int32, (ROWS, LANES), 1)
    results = []
    for j in range(count):
        part = mixed[:, j * LANES : (j + 1) * LANES]
        before = pltpu.roll(part[:ROWS], 1, axis=1)
        after = pltpu.roll(part[2 * ROWS :], LANES - 1, axis=1)
        conv = part[ROWS : 2 * ROWS] + bias
        conv = conv + jnp.where(lane == 0, 0.0, before) + jnp.where(lane == LANES - 1, 0.0, after)
        results.append(jnp.tanh(conv))
    return results


def store_split(high, low, slot, plane, value):
    h, l = split(value)
    high[slot, plane * ROWS : (plane + 1) * ROWS, :] = h
    low[slot, plane * ROWS : (plane + 1) * ROWS, :] = l


def block_kernel(by_channel, forcing, first_step, flags, pair, middle, other_pair, packed, *refs):
    if forcing:
        beside, out, minus, wide, narrow, taps, state, high, low, coarse = refs
    else:
        out, wide, narrow, taps, state, high, low = refs
    planes = 3 * SLAB
    steps = wide.shape[0]
    scale = {0: flags[1].astype(jnp.float32), 2: flags[2].astype(jnp.float32)}

    def inside(plane, value):
        side = plane // SLAB
        return value * scale[side] if side != 1 else value

    def fetch(source, plane):
        return source[:, plane].reshape(ROWS, LANES) if by_channel else source[plane]

    paired_above = flags[7] == 0
    for plane in range(planes):
        side, at = plane // SLAB, plane % SLAB
        if side == 1:
            value = fetch(middle, at)
        else:
            above, below = (pair, other_pair) if side == 2 else (other_pair, pair)
            value = jnp.where(paired_above, fetch(above, at), fetch(below, at))
        value = inside(plane, value)
        state[plane] = value
        store_split(high, low, 0, plane, value)
    for step in range(steps):
        build_band(packed.at[first_step + step], wide.at[step], narrow.at[step], taps.at[step])
        first, last = step + 1, planes - 1 - step
        now, later = step % 2, (step + 1) % 2
        bias = offsets(packed.at[first_step + step])
        for at in range(first, last, 2):
            outs = activations(high.at[now], low.at[now], wide[step], narrow[step], bias, at, 2)
            for plane, change in zip((at, at + 1), outs):
                old = state[plane]
                value = inside(plane, old + FINE * change)
                own = SLAB <= plane < 2 * SLAB
                if forcing and step == 0 and own:
                    coarse[plane - SLAB] = old + COARSE * change
                if step < steps - 1:
                    state[plane] = value
                    store_split(high, low, later, plane, value)
                else:
                    if not forcing:
                        out[plane - SLAB] = value
                        continue
                    at_home = plane - SLAB
                    minus[at_home] = value - coarse[at_home] * flags[3].astype(jnp.float32)
                    other = beside[at_home]
                    less = jnp.where(flags[6] == 1, other, value - other)
                    out[at_home] = jnp.where(flags[0] == 0, less, value)


VMEM = pl.BlockSpec(memory_space=pltpu.VMEM)
SMEM = pl.BlockSpec(memory_space=pltpu.SMEM)


def call(kernel, outs, scratch, flops, flags, *arrays):
    return pl.pallas_call(
        kernel,
        in_specs=[SMEM] + [VMEM] * len(arrays),
        out_specs=[VMEM] * len(outs),
        out_shape=[jax.ShapeDtypeStruct(shape, jnp.float32) for shape in outs],
        scratch_shapes=scratch,
        compiler_params=pltpu.CompilerParams(vmem_limit_bytes=VMEM_LIMIT),
        cost_estimate=pl.CostEstimate(flops=flops, bytes_accessed=2000000, transcendentals=0),
    )(flags, *arrays)


def plane_shape(count):
    return (count, ROWS, LANES)


def matrices(steps):
    return [
        pltpu.VMEM((steps, BAND, BAND), jnp.bfloat16),
        pltpu.VMEM((steps, BAND, BAND), jnp.bfloat16),
        pltpu.VMEM((steps, 2 * KERNEL_ROWS, BAND), jnp.float32),
    ]


def states(planes):
    return [
        pltpu.VMEM((planes, ROWS, LANES), jnp.float32),
        pltpu.VMEM((2, planes * ROWS, LANES), jnp.bfloat16),
        pltpu.VMEM((2, planes * ROWS, LANES), jnp.bfloat16),
    ]


def run_block(flags, pair, middle, other_pair, packed, steps, by_channel, beside=()):
    forcing = len(beside) > 0
    scratch = matrices(steps) + states(3 * SLAB)
    outs = [plane_shape(SLAB)]
    if forcing:
        scratch.append(pltpu.VMEM(plane_shape(SLAB), jnp.float32))
        outs = outs * 2
    kernel = functools.partial(block_kernel, by_channel, forcing, steps if forcing else 0)
    return call(kernel, outs, scratch, 4000000000, flags, pair, middle, other_pair, packed, *beside)


def meet_kernel(flags, own, swapped, mine, near, rim, paid):
    lower = flags[0] == 0

    def even(a, b):
        return jnp.where(lower, own[a], swapped[b])

    for j in range(2):
        odd = jnp.where(lower, swapped[j], own[2 + j])
        near[j] = jnp.where(lower, swapped[2 + j], own[j])
        mine[j] = odd
        paid[3 + j] = odd
    for j in range(3):
        paid[j] = even(j, 1 + j)
    outer = even(0, 3)
    mine[2] = outer
    rim[0] = outer


def pay_kernel(flags, paid, far, out):
    lower = flags[0] == 0
    out[0] = jnp.where(lower, far[2], paid[0])
    out[1] = jnp.where(lower, paid[0], paid[1])
    out[2] = jnp.where(lower, paid[1], paid[2])
    out[3] = jnp.where(lower, paid[2], far[2])
    for j in range(2):
        out[4 + j] = paid[3 + j]


def sweep_kernel(first, final, step, flags, mine, near, far, paid, *refs):
    lower = flags[0] == 0
    if first:
        edge, *refs = refs
        forcing = [
            lambda: jnp.where(lower, edge[0], paid[0]),
            lambda: jnp.where(lower, paid[0], paid[1]),
            lambda: jnp.where(lower, paid[1], paid[2]),
            lambda: jnp.where(lower, paid[2], edge[0]),
            lambda: paid[3],
            lambda: paid[4],
        ]
    else:
        forcing = [functools.partial(lambda p: paid[p], p) for p in range(6)]
    packed, pair, last, wide, narrow, taps, state, high, low = refs
    left_scale = jnp.where(lower, flags[1], 1).astype(jnp.float32)
    right_scale = jnp.where(lower, 1, flags[2]).astype(jnp.float32)
    for j in range(2):
        values = {
            j: jnp.where(lower, far[j], near[j]) * left_scale,
            2 + j: mine[j],
            4 + j: jnp.where(lower, near[j], far[j]) * right_scale,
        }
        for plane, value in values.items():
            state[plane] = value
            store_split(high, low, 0, plane, value)
    for s in range(2):
        build_band(packed.at[step + s], wide.at[s], narrow.at[s], taps.at[s])
    bias = offsets(packed.at[step])
    for at in (1, 3):
        outs = activations(high.at[0], low.at[0], wide[0], narrow[0], bias, at, 2)
        for plane, change in zip((at, at + 1), outs):
            value = state[plane] + COARSE * change + forcing[plane - 1]()
            if plane == 1:
                value = value * left_scale
            if plane == 4:
                value = value * right_scale
            state[plane] = value
            store_split(high, low, 1, plane, value)
            if plane in (2, 3):
                pair[plane - 2] = value
    outs = activations(high.at[1], low.at[1], wide[1], narrow[1], offsets(packed.at[step + 1]), 2, 2)
    for j, change in enumerate(outs):
        value = state[2 + j] + COARSE * change + forcing[4 + j]()
        if final:
            even = pair[j]
            pair[j] = jnp.where(lower, even, value)
            last[j] = jnp.where(lower, value, even)
        else:
            pair[2 + j] = value
            last[j] = value


def run_sweep(first, final, step, flags, *arrays):
    kernel = functools.partial(sweep_kernel, first, final, step)
    outs = [plane_shape(2 if final else 4), plane_shape(2)]
    return call(kernel, outs, matrices(2) + states(6), 900000000, flags, *arrays)


def finish_kernel(flags, kept, got, second, second_got, fourth, fourth_got, home, out):
    lower, chip = flags[0] == 0, flags[4]

    def early(pair, other, plane):
        j = plane % 2
        low = jnp.where(lower, pair[j], other[2 + j])
        return low if plane < 2 else jnp.where(lower, other[j], pair[2 + j])

    for plane in range(SLAB):
        j = plane % 2
        value = jnp.where(lower, kept[j], got[j]) if plane < 2 else jnp.where(lower, got[j], kept[j])
        value = jnp.where(chip == 1, early(second, second_got, plane), value)
        value = jnp.where(chip == 2, early(fourth, fourth_got, plane), value)
        value = jnp.where(chip == 0, home[plane], value)
        out[0, :, plane] = value.reshape(out.shape[1], CELLS, LANES)


def residual_kernel(flags, beside, home, out):
    for plane in range(SLAB):
        value = home[plane]
        value = jnp.where(flags[0] == 0, value, value - beside[plane])
        value = jnp.where(flags[5] == 0, 0.0, value)
        out[0, :, plane] = value.reshape(out.shape[1], CELLS, LANES)


def on_device(layers, slabs, initial, guess, weights, bias):
    layer = lax.axis_index("layer")
    slab = lax.axis_index("space")
    core = layer % 2
    lower = core == 0

    def send(array, target):
        pairs = []
        for l in range(layers):
            for s in range(slabs):
                to_l, to_s = target(l, s)
                pairs.append((l * slabs + s, (to_l % layers) * slabs + to_s % slabs))
        return lax.ppermute(array, ("layer", "space"), pairs)

    def paired(l, s):
        return l, s ^ 1

    def other_paired(l, s):
        to_s = s + 1 if s % 2 else s - 1
        return (l, to_s) if 0 <= to_s < slabs else (l ^ 1, s)

    def across(l, s):
        return l ^ 1, s

    def chips(flip, l):
        return 2 * (l // 2 ^ flip) + l % 2

    def zigzag(l, s, flip=0):
        to_s = s - 1 if l % 2 == 0 else s + 1
        if 0 <= to_s < slabs:
            return chips(flip, l ^ 1), to_s
        return chips(flip or 1, l), s

    def zigzag_flipped(l, s):
        return zigzag(l, s, 3)

    def flipped(flip):
        return lambda l, s: (chips(flip, l), s)

    def shifted(by):
        return lambda l, s: (l + by, s)

    def far_chips(l, s):
        return flipped(2)(l, s) if l // 2 in (1, 3) else (l, s)

    flags = [core, slab > 0, slab < slabs - 1, layer < layers - 1, layer // 2, layer, layer == layers - 2, slab % 2]
    flags = jnp.stack(flags).astype(jnp.int32)
    group = weights.shape[0]

    start = jnp.where(layer == layers - 1, initial, guess[0])
    pair, other_pair = send(start, paired), send(start, other_paired)
    taps = jnp.pad(weights, ((0, 0), (0, 0), (0, BIAS_AT - weights.shape[2])))
    raw = jnp.concatenate([taps, jnp.broadcast_to(bias[:, :, None], bias.shape + (LANES,))], 2)
    raw_here = jnp.concatenate([send(raw, shifted(-1)), send(raw, shifted(-2))], 0)

    def pack(piece):
        count, channels, _ = piece.shape
        kernel = piece[:, :, : TAPS**3 * channels].reshape(count, channels, TAPS, TAPS, TAPS, channels)
        kernel = kernel.transpose(0, 3, 4, 1, 2, 5).reshape(count, KERNEL_ROWS, TAPS * channels)
        kernel = jnp.pad(kernel, ((0, 0), (0, 0), (0, LANES - TAPS * channels)))
        return jnp.concatenate([kernel, piece[:, :, BIAS_AT:]], 1)

    packed = pack(raw_here)
    coarse, _ = lax.optimization_barrier((raw[:1], packed))
    coarse_swapped = send(coarse, across)
    coarse = jnp.where(
        lower, jnp.concatenate([coarse, coarse_swapped], 0), jnp.concatenate([coarse_swapped, coarse], 0)
    )
    (relaxed,) = run_block(flags, pair, start, other_pair, packed, group, by_channel=True)

    pair, other_pair = send(relaxed, paired), send(relaxed, other_paired)
    beside = send(relaxed, across)
    sweep = pack(jnp.concatenate([send(coarse, flipped(2)), send(coarse, flipped(1)), coarse], 0))
    pair, sweep = lax.optimization_barrier((pair, sweep))
    home, forced = run_block(flags, pair, relaxed, other_pair, packed, group, by_channel=False, beside=(beside,))

    swapped = send(forced, across)
    outs = [plane_shape(count) for count in (3, 2, 1, 5)]
    mine, near, rim, paid = call(meet_kernel, outs, [], 0, flags, forced, swapped)
    far, edge = send(mine, zigzag), send(rim, zigzag_flipped)
    paid_in = send(paid, flipped(3))
    home = send(home, shifted(2))
    far, edge = lax.optimization_barrier((far, edge))
    (pay,) = call(pay_kernel, [plane_shape(6)], [], 0, flags, paid, far)
    pay_two = send(pay, far_chips)
    second, last = run_sweep(True, False, 0, flags, mine, near, far, paid_in, edge, sweep)

    near, far = send(last, across), send(last, zigzag)
    pay, _ = lax.optimization_barrier((pay, paid_in))
    pay_three = send(pay, flipped(1))
    far, home = lax.optimization_barrier((far, home))
    fourth, last = run_sweep(False, False, 2, flags, last, near, far, pay_two, sweep)

    second, _ = lax.optimization_barrier((second, far))
    second = send(second, far_chips)
    near, far = send(last, across), send(last, zigzag)
    fourth = send(fourth, flipped(1))
    out = (1, initial.shape[0], SLAB, CELLS, LANES)
    kept, give = run_sweep(False, True, 4, flags, last, near, far, pay_three, sweep)

    second, fourth, give = lax.optimization_barrier((second, fourth, give))
    got, second_got, fourth_got = send(give, across), send(second, across), send(fourth, across)
    (residual,) = call(residual_kernel, [out], [], 0, flags, beside, home)
    (corrected,) = call(
        finish_kernel, [out], [], 0, flags, kept, got, second, second_got, fourth, fourth_got, home
    )
    return corrected, residual


def solution(mesh):
    layers, slabs = mesh.shape["layer"], mesh.shape["space"]
    in_specs = (
        P(None, "space", None, None),
        P("layer", None, "space", None, None),
        P("layer", None, None),
        P("layer", None),
    )
    out_specs = (P("layer", None, "space", None, None), P("layer", None, "space", None, None))
    return jax.shard_map(
        functools.partial(on_device, layers, slabs),
        mesh=mesh,
        in_specs=in_specs,
        out_specs=out_specs,
        check_vma=False,
    )
```

```python
import functools

import jax
import jax.numpy as jnp
from jax import lax
from jax.experimental import pallas as pl
from jax.experimental.pallas import tpu as pltpu
from jax.sharding import PartitionSpec as P

FINE = 0.25
COARSE = 1.0
LANES = 128
ROWS = 128
TAPS = 3
BAND = TAPS * ROWS
SLAB = 4
CELLS = 16
KERNEL_ROWS = 72
PACKED_ROWS = 80
BIAS_AT = 256
VMEM_LIMIT = 16 * 1024 * 1024


def split(value):
    high = value.astype(jnp.bfloat16)
    low = (value - high.astype(jnp.float32)).astype(jnp.bfloat16)
    return high, low


def build_kernel(flags, packed, out, taps):
    lane = lax.broadcasted_iota(jnp.int32, (LANES, BAND), 1)
    spread = jnp.where(lane // CELLS == lax.broadcasted_iota(jnp.int32, (LANES, BAND), 0), 1.0, 0.0)
    spread = spread.astype(jnp.bfloat16)
    row = lax.broadcasted_iota(jnp.int32, (CELLS, BAND), 0)
    offset = lax.broadcasted_iota(jnp.int32, (CELLS, BAND), 1) % CELLS - row
    blocks = BAND // CELLS
    for step in range(out.shape[0]):
        high, low = split(packed[step, :KERNEL_ROWS, :])
        both = jnp.concatenate([high, low], axis=0)
        taps[step] = jnp.dot(both, spread, preferred_element_type=jnp.float32)
        for part in range(2):
            for block in range(blocks):
                total = jnp.zeros((CELLS, BAND), jnp.float32)
                for tap in range(TAPS):
                    at = part * KERNEL_ROWS + tap * blocks + block
                    total = jnp.where(offset == tap - 1, taps[step, at : at + 1, :], total)
                total = total.astype(jnp.bfloat16)
                rows = slice(block * CELLS, (block + 1) * CELLS)
                out[step, rows, part * BAND : (part + 1) * BAND] = total
                if part == 0:
                    out[step, rows, 2 * BAND :] = total


def offsets(packed):
    rows = [jnp.broadcast_to(packed[at : at + 1, :], (CELLS, LANES)) for at in range(KERNEL_ROWS, PACKED_ROWS)]
    return jnp.concatenate(rows, axis=0)


def window(planes, at, count):
    pieces = [planes[(p - 1) * ROWS : (p + 2) * ROWS, :] for p in range(at, at + count)]
    return pieces[0] if count == 1 else jnp.concatenate(pieces, axis=1)


def activations(high, low, bands, bias, at, count):
    right = window(high, at, count)
    right = jnp.concatenate([right, right, window(low, at, count)], axis=0)
    mixed = jnp.dot(bands, right, preferred_element_type=jnp.float32)
    lane = lax.broadcasted_iota(jnp.int32, (ROWS, LANES), 1)
    results = []
    for j in range(count):
        part = mixed[:, j * LANES : (j + 1) * LANES]
        before = pltpu.roll(part[:ROWS], 1, axis=1)
        after = pltpu.roll(part[2 * ROWS :], LANES - 1, axis=1)
        conv = part[ROWS : 2 * ROWS] + bias
        conv = conv + jnp.where(lane == 0, 0.0, before) + jnp.where(lane == LANES - 1, 0.0, after)
        results.append(jnp.tanh(conv))
    return results


def store_split(high, low, slot, plane, value):
    h, l = split(value)
    high[slot, plane * ROWS : (plane + 1) * ROWS, :] = h
    low[slot, plane * ROWS : (plane + 1) * ROWS, :] = l


def block_kernel(by_channel, forcing, flags, pair, middle, other_pair, packed, bands, *refs):
    if forcing:
        beside, out, minus, state, high, low, coarse = refs
    else:
        out, state, high, low = refs
    planes = 3 * SLAB
    steps = bands.shape[0]
    scale = {0: flags[1].astype(jnp.float32), 2: flags[2].astype(jnp.float32)}

    def inside(plane, value):
        side = plane // SLAB
        return value * scale[side] if side != 1 else value

    def fetch(source, plane):
        return source[:, plane].reshape(ROWS, LANES) if by_channel else source[plane]

    paired_above = flags[7] == 0
    for plane in range(planes):
        side, at = plane // SLAB, plane % SLAB
        if side == 1:
            value = fetch(middle, at)
        else:
            above, below = (pair, other_pair) if side == 2 else (other_pair, pair)
            value = jnp.where(paired_above, fetch(above, at), fetch(below, at))
        value = inside(plane, value)
        state[plane] = value
        store_split(high, low, 0, plane, value)
    for step in range(steps):
        first, last = step + 1, planes - 1 - step
        now, later = step % 2, (step + 1) % 2
        bias = offsets(packed.at[step])
        for at in range(first, last, 2):
            outs = activations(high.at[now], low.at[now], bands[step], bias, at, 2)
            for plane, change in zip((at, at + 1), outs):
                old = state[plane]
                value = inside(plane, old + FINE * change)
                own = SLAB <= plane < 2 * SLAB
                if forcing and step == 0 and own:
                    coarse[plane - SLAB] = old + COARSE * change
                if step < steps - 1:
                    state[plane] = value
                    store_split(high, low, later, plane, value)
                else:
                    if not forcing:
                        out[plane - SLAB] = value
                        continue
                    at_home = plane - SLAB
                    minus[at_home] = value - coarse[at_home] * flags[3].astype(jnp.float32)
                    other = beside[at_home]
                    less = jnp.where(flags[6] == 1, other, value - other)
                    out[at_home] = jnp.where(flags[0] == 0, less, value)


VMEM = pl.BlockSpec(memory_space=pltpu.VMEM)
SMEM = pl.BlockSpec(memory_space=pltpu.SMEM)


def call(kernel, outs, scratch, flops, flags, *arrays):
    return pl.pallas_call(
        kernel,
        in_specs=[SMEM] + [VMEM] * len(arrays),
        out_specs=[VMEM] * len(outs),
        out_shape=[shape if hasattr(shape, "dtype") else jax.ShapeDtypeStruct(shape, jnp.float32) for shape in outs],
        scratch_shapes=scratch,
        compiler_params=pltpu.CompilerParams(vmem_limit_bytes=VMEM_LIMIT),
        cost_estimate=pl.CostEstimate(flops=flops, bytes_accessed=2000000, transcendentals=0),
    )(flags, *arrays)


def plane_shape(count):
    return (count, ROWS, LANES)


def build(flags, packed):
    steps = packed.shape[0]
    scratch = [pltpu.VMEM((steps, 2 * KERNEL_ROWS, BAND), jnp.float32)]
    shape = jax.ShapeDtypeStruct((steps, BAND, 3 * BAND), jnp.bfloat16)
    return call(build_kernel, [shape], scratch, steps * 20000000, flags, packed)[0]


def states(planes):
    return [
        pltpu.VMEM((planes, ROWS, LANES), jnp.float32),
        pltpu.VMEM((2, planes * ROWS, LANES), jnp.bfloat16),
        pltpu.VMEM((2, planes * ROWS, LANES), jnp.bfloat16),
    ]


def run_block(flags, pair, middle, other_pair, packed, bands, by_channel, beside=()):
    forcing = len(beside) > 0
    scratch = states(3 * SLAB)
    outs = [plane_shape(SLAB)]
    if forcing:
        scratch.append(pltpu.VMEM(plane_shape(SLAB), jnp.float32))
        outs = outs * 2
    kernel = functools.partial(block_kernel, by_channel, forcing)
    return call(kernel, outs, scratch, 4000000000, flags, pair, middle, other_pair, packed, bands, *beside)


def meet_kernel(flags, own, swapped, mine, near, rim, paid):
    lower = flags[0] == 0

    def even(a, b):
        return jnp.where(lower, own[a], swapped[b])

    for j in range(2):
        odd = jnp.where(lower, swapped[j], own[2 + j])
        near[j] = jnp.where(lower, swapped[2 + j], own[j])
        mine[j] = odd
        paid[3 + j] = odd
    for j in range(3):
        paid[j] = even(j, 1 + j)
    outer = even(0, 3)
    mine[2] = outer
    rim[0] = outer


def pay_kernel(flags, paid, far, out):
    lower = flags[0] == 0
    out[0] = jnp.where(lower, far[2], paid[0])
    out[1] = jnp.where(lower, paid[0], paid[1])
    out[2] = jnp.where(lower, paid[1], paid[2])
    out[3] = jnp.where(lower, paid[2], far[2])
    for j in range(2):
        out[4 + j] = paid[3 + j]


def sweep_kernel(first, final, step, flags, mine, near, far, paid, *refs):
    lower = flags[0] == 0
    if first:
        edge, *refs = refs
        forcing = [
            lambda: jnp.where(lower, edge[0], paid[0]),
            lambda: jnp.where(lower, paid[0], paid[1]),
            lambda: jnp.where(lower, paid[1], paid[2]),
            lambda: jnp.where(lower, paid[2], edge[0]),
            lambda: paid[3],
            lambda: paid[4],
        ]
    else:
        forcing = [functools.partial(lambda p: paid[p], p) for p in range(6)]
    packed, bands, pair, last, state, high, low = refs
    left_scale = jnp.where(lower, flags[1], 1).astype(jnp.float32)
    right_scale = jnp.where(lower, 1, flags[2]).astype(jnp.float32)
    for j in range(2):
        values = {
            j: jnp.where(lower, far[j], near[j]) * left_scale,
            2 + j: mine[j],
            4 + j: jnp.where(lower, near[j], far[j]) * right_scale,
        }
        for plane, value in values.items():
            state[plane] = value
            store_split(high, low, 0, plane, value)
    bias = offsets(packed.at[step])
    for at in (1, 3):
        outs = activations(high.at[0], low.at[0], bands[step], bias, at, 2)
        for plane, change in zip((at, at + 1), outs):
            value = state[plane] + COARSE * change + forcing[plane - 1]()
            if plane == 1:
                value = value * left_scale
            if plane == 4:
                value = value * right_scale
            state[plane] = value
            store_split(high, low, 1, plane, value)
            if plane in (2, 3):
                pair[plane - 2] = value
    outs = activations(high.at[1], low.at[1], bands[step + 1], offsets(packed.at[step + 1]), 2, 2)
    for j, change in enumerate(outs):
        value = state[2 + j] + COARSE * change + forcing[4 + j]()
        if final:
            even = pair[j]
            pair[j] = jnp.where(lower, even, value)
            last[j] = jnp.where(lower, value, even)
        else:
            pair[2 + j] = value
            last[j] = value


def run_sweep(first, final, step, flags, *arrays):
    kernel = functools.partial(sweep_kernel, first, final, step)
    outs = [plane_shape(2 if final else 4), plane_shape(2)]
    return call(kernel, outs, states(6), 900000000, flags, *arrays)


def finish_kernel(flags, kept, got, second, second_got, fourth, fourth_got, home, out):
    lower, chip = flags[0] == 0, flags[4]

    def early(pair, other, plane):
        j = plane % 2
        low = jnp.where(lower, pair[j], other[2 + j])
        return low if plane < 2 else jnp.where(lower, other[j], pair[2 + j])

    for plane in range(SLAB):
        j = plane % 2
        value = jnp.where(lower, kept[j], got[j]) if plane < 2 else jnp.where(lower, got[j], kept[j])
        value = jnp.where(chip == 1, early(second, second_got, plane), value)
        value = jnp.where(chip == 2, early(fourth, fourth_got, plane), value)
        value = jnp.where(chip == 0, home[plane], value)
        out[0, :, plane] = value.reshape(out.shape[1], CELLS, LANES)


def residual_kernel(flags, beside, home, out):
    for plane in range(SLAB):
        value = home[plane]
        value = jnp.where(flags[0] == 0, value, value - beside[plane])
        value = jnp.where(flags[5] == 0, 0.0, value)
        out[0, :, plane] = value.reshape(out.shape[1], CELLS, LANES)


def on_device(layers, slabs, initial, guess, weights, bias):
    layer = lax.axis_index("layer")
    slab = lax.axis_index("space")
    core = layer % 2
    lower = core == 0

    def send(array, target):
        pairs = []
        for l in range(layers):
            for s in range(slabs):
                to_l, to_s = target(l, s)
                pairs.append((l * slabs + s, (to_l % layers) * slabs + to_s % slabs))
        return lax.ppermute(array, ("layer", "space"), pairs)

    def paired(l, s):
        return l, s ^ 1

    def other_paired(l, s):
        to_s = s + 1 if s % 2 else s - 1
        return (l, to_s) if 0 <= to_s < slabs else (l ^ 1, s)

    def across(l, s):
        return l ^ 1, s

    def chips(flip, l):
        return 2 * (l // 2 ^ flip) + l % 2

    def zigzag(l, s, flip=0, end=1):
        to_s = s - 1 if l % 2 == 0 else s + 1
        if 0 <= to_s < slabs:
            return chips(flip, l ^ 1), to_s
        return chips(flip or end, l), s

    def zigzag_flipped(l, s):
        return zigzag(l, s, 3)

    def zigzag_on(l, s):
        return zigzag(l, s, 0, 3)

    def flipped(flip):
        return lambda l, s: (chips(flip, l), s)

    def shifted(by):
        return lambda l, s: (l + by, s)

    def far_chips(l, s):
        return flipped(2)(l, s) if l // 2 in (1, 3) else (l, s)

    flags = [core, slab > 0, slab < slabs - 1, layer < layers - 1, layer // 2, layer, layer == layers - 2, slab % 2]
    flags = jnp.stack(flags).astype(jnp.int32)
    group = weights.shape[0]

    start = jnp.where(layer == layers - 1, initial, guess[0])
    pair, other_pair = send(start, paired), send(start, other_paired)
    taps = jnp.pad(weights, ((0, 0), (0, 0), (0, BIAS_AT - weights.shape[2])))
    raw = jnp.concatenate([taps, jnp.broadcast_to(bias[:, :, None], bias.shape + (LANES,))], 2)
    raw_here = jnp.concatenate([send(raw, shifted(-1)), send(raw, shifted(-2))], 0)

    def pack(piece):
        count, channels, _ = piece.shape
        kernel = piece[:, :, : TAPS**3 * channels].reshape(count, channels, TAPS, TAPS, TAPS, channels)
        kernel = kernel.transpose(0, 3, 4, 1, 2, 5).reshape(count, KERNEL_ROWS, TAPS * channels)
        kernel = jnp.pad(kernel, ((0, 0), (0, 0), (0, LANES - TAPS * channels)))
        return jnp.concatenate([kernel, piece[:, :, BIAS_AT:]], 1)

    packed = pack(raw_here)
    bands = build(flags, packed[:group])
    coarse, _ = lax.optimization_barrier((raw[:1], packed))
    coarse_swapped = send(coarse, across)
    coarse = jnp.where(
        lower, jnp.concatenate([coarse, coarse_swapped], 0), jnp.concatenate([coarse_swapped, coarse], 0)
    )
    (relaxed,) = run_block(flags, pair, start, other_pair, packed[:group], bands, by_channel=True)

    pair, other_pair = send(relaxed, paired), send(relaxed, other_paired)
    beside = send(relaxed, across)
    sweep = pack(jnp.concatenate([send(coarse, flipped(2)), send(coarse, flipped(1)), coarse], 0))
    later, _ = lax.optimization_barrier((packed[group:], relaxed))
    bands = build(flags, later)
    pair, sweep = lax.optimization_barrier((pair, sweep))
    home, forced = run_block(flags, pair, relaxed, other_pair, later, bands, by_channel=False, beside=(beside,))

    swapped = send(forced, across)
    outs = [plane_shape(count) for count in (3, 2, 1, 5)]
    mine, near, rim, paid = call(meet_kernel, outs, [], 0, flags, forced, swapped)
    far, edge = send(mine, zigzag), send(rim, zigzag_flipped)
    sweep, _ = lax.optimization_barrier((sweep, near))
    bands = build(flags, sweep)
    paid_in = send(paid, shifted(-2))
    home = send(home, shifted(2))
    far, edge, bands = lax.optimization_barrier((far, edge, bands))
    (pay,) = call(pay_kernel, [plane_shape(6)], [], 0, flags, paid, far)
    pay_two = send(pay, far_chips)
    paid_in, home = lax.optimization_barrier((paid_in, home))
    second, last = run_sweep(True, False, 0, flags, mine, near, far, paid_in, edge, sweep, bands)

    near, far = send(last, across), send(last, zigzag_on)
    pay, _ = lax.optimization_barrier((pay, paid_in))
    pay_three = send(pay, flipped(1))
    fourth, last = run_sweep(False, False, 2, flags, last, near, far, pay_two, sweep, bands)

    second, _ = lax.optimization_barrier((second, far))
    second = send(second, far_chips)
    near, far = send(last, across), send(last, zigzag_on)
    fourth = send(fourth, flipped(1))
    out = (1, initial.shape[0], SLAB, CELLS, LANES)
    kept, give = run_sweep(False, True, 4, flags, last, near, far, pay_three, sweep, bands)

    second, fourth, give = lax.optimization_barrier((second, fourth, give))
    got, second_got, fourth_got = send(give, across), send(second, across), send(fourth, across)
    (residual,) = call(residual_kernel, [out], [], 0, flags, beside, home)
    (corrected,) = call(
        finish_kernel, [out], [], 0, flags, kept, got, second, second_got, fourth, fourth_got, home
    )
    return corrected, residual


def solution(mesh):
    layers, slabs = mesh.shape["layer"], mesh.shape["space"]
    in_specs = (
        P(None, "space", None, None),
        P("layer", None, "space", None, None),
        P("layer", None, None),
        P("layer", None),
    )
    out_specs = (P("layer", None, "space", None, None), P("layer", None, "space", None, None))
    return jax.shard_map(
        functools.partial(on_device, layers, slabs),
        mesh=mesh,
        in_specs=in_specs,
        out_specs=out_specs,
        check_vma=False,
    )
```

```python
import functools

import jax
import jax.numpy as jnp
from jax import lax
from jax.experimental import pallas as pl
from jax.experimental.pallas import tpu as pltpu
from jax.sharding import PartitionSpec as P

FINE = 0.25
COARSE = 1.0
LANES = 128
ROWS = 128
TAPS = 3
BAND = TAPS * ROWS
SLAB = 4
CELLS = 16
KERNEL_ROWS = 72
PACKED_ROWS = 80
BIAS_AT = 256
VMEM_LIMIT = 16 * 1024 * 1024


def split(value):
    high = value.astype(jnp.bfloat16)
    low = (value - high.astype(jnp.float32)).astype(jnp.bfloat16)
    return high, low


def build_kernel(flags, packed, out, taps):
    lane = lax.broadcasted_iota(jnp.int32, (LANES, BAND), 1)
    spread = jnp.where(lane // CELLS == lax.broadcasted_iota(jnp.int32, (LANES, BAND), 0), 1.0, 0.0)
    spread = spread.astype(jnp.bfloat16)
    row = lax.broadcasted_iota(jnp.int32, (CELLS, BAND), 0)
    offset = lax.broadcasted_iota(jnp.int32, (CELLS, BAND), 1) % CELLS - row
    blocks = BAND // CELLS
    for step in range(out.shape[0]):
        high, low = split(packed[step, :KERNEL_ROWS, :])
        both = jnp.concatenate([high, low], axis=0)
        taps[step] = jnp.dot(both, spread, preferred_element_type=jnp.float32)
        for part in range(2):
            for block in range(blocks):
                total = jnp.zeros((CELLS, BAND), jnp.float32)
                for tap in range(TAPS):
                    at = part * KERNEL_ROWS + tap * blocks + block
                    total = jnp.where(offset == tap - 1, taps[step, at : at + 1, :], total)
                total = total.astype(jnp.bfloat16)
                rows = slice(block * CELLS, (block + 1) * CELLS)
                out[step, rows, part * BAND : (part + 1) * BAND] = total
                if part == 0:
                    out[step, rows, 2 * BAND :] = total


def offsets(packed):
    rows = [jnp.broadcast_to(packed[at : at + 1, :], (CELLS, LANES)) for at in range(KERNEL_ROWS, PACKED_ROWS)]
    return jnp.concatenate(rows, axis=0)


def window(planes, at, count):
    pieces = [planes[(p - 1) * ROWS : (p + 2) * ROWS, :] for p in range(at, at + count)]
    return pieces[0] if count == 1 else jnp.concatenate(pieces, axis=1)


def activations(high, low, bands, bias, at, count):
    right = window(high, at, count)
    right = jnp.concatenate([right, right, window(low, at, count)], axis=0)
    mixed = jnp.dot(bands, right, preferred_element_type=jnp.float32)
    lane = lax.broadcasted_iota(jnp.int32, (ROWS, LANES), 1)
    results = []
    for j in range(count):
        part = mixed[:, j * LANES : (j + 1) * LANES]
        before = pltpu.roll(part[:ROWS], 1, axis=1)
        after = pltpu.roll(part[2 * ROWS :], LANES - 1, axis=1)
        conv = part[ROWS : 2 * ROWS] + bias
        conv = conv + jnp.where(lane == 0, 0.0, before) + jnp.where(lane == LANES - 1, 0.0, after)
        results.append(jnp.tanh(conv))
    return results


def store_split(high, low, slot, plane, value):
    h, l = split(value)
    high[slot, plane * ROWS : (plane + 1) * ROWS, :] = h
    low[slot, plane * ROWS : (plane + 1) * ROWS, :] = l


def block_kernel(by_channel, forcing, flags, pair, middle, other_pair, packed, bands, *refs):
    if forcing:
        beside, out, minus, state, high, low, coarse = refs
    else:
        out, state, high, low = refs
    planes = 3 * SLAB
    steps = bands.shape[0]
    scale = {0: flags[1].astype(jnp.float32), 2: flags[2].astype(jnp.float32)}

    def inside(plane, value):
        side = plane // SLAB
        return value * scale[side] if side != 1 else value

    def fetch(source, plane):
        return source[:, plane].reshape(ROWS, LANES) if by_channel else source[plane]

    paired_above = flags[7] == 0
    for plane in range(planes):
        side, at = plane // SLAB, plane % SLAB
        if side == 1:
            value = fetch(middle, at)
        else:
            above, below = (pair, other_pair) if side == 2 else (other_pair, pair)
            value = jnp.where(paired_above, fetch(above, at), fetch(below, at))
        value = inside(plane, value)
        state[plane] = value
        store_split(high, low, 0, plane, value)
    for step in range(steps):
        first, last = step + 1, planes - 1 - step
        now, later = step % 2, (step + 1) % 2
        bias = offsets(packed.at[step])
        for at in range(first, last, 2):
            outs = activations(high.at[now], low.at[now], bands[step], bias, at, 2)
            for plane, change in zip((at, at + 1), outs):
                old = state[plane]
                value = inside(plane, old + FINE * change)
                own = SLAB <= plane < 2 * SLAB
                if forcing and step == 0 and own:
                    coarse[plane - SLAB] = old + COARSE * change
                if step < steps - 1:
                    state[plane] = value
                    store_split(high, low, later, plane, value)
                else:
                    if not forcing:
                        out[plane - SLAB] = value
                        continue
                    at_home = plane - SLAB
                    minus[at_home] = value - coarse[at_home] * flags[3].astype(jnp.float32)
                    other = beside[at_home]
                    less = jnp.where(flags[6] == 1, other, value - other)
                    out[at_home] = jnp.where(flags[0] == 0, less, value)


VMEM = pl.BlockSpec(memory_space=pltpu.VMEM)
SMEM = pl.BlockSpec(memory_space=pltpu.SMEM)


def call(kernel, outs, scratch, flops, flags, *arrays):
    return pl.pallas_call(
        kernel,
        in_specs=[SMEM] + [VMEM] * len(arrays),
        out_specs=[VMEM] * len(outs),
        out_shape=[shape if hasattr(shape, "dtype") else jax.ShapeDtypeStruct(shape, jnp.float32) for shape in outs],
        scratch_shapes=scratch,
        compiler_params=pltpu.CompilerParams(vmem_limit_bytes=VMEM_LIMIT),
        cost_estimate=pl.CostEstimate(flops=flops, bytes_accessed=2000000, transcendentals=0),
    )(flags, *arrays)


def plane_shape(count):
    return (count, ROWS, LANES)


def build(flags, packed):
    steps = packed.shape[0]
    scratch = [pltpu.VMEM((steps, 2 * KERNEL_ROWS, BAND), jnp.float32)]
    shape = jax.ShapeDtypeStruct((steps, BAND, 3 * BAND), jnp.bfloat16)
    return call(build_kernel, [shape], scratch, steps * 20000000, flags, packed)[0]


def states(planes):
    return [
        pltpu.VMEM((planes, ROWS, LANES), jnp.float32),
        pltpu.VMEM((2, planes * ROWS, LANES), jnp.bfloat16),
        pltpu.VMEM((2, planes * ROWS, LANES), jnp.bfloat16),
    ]


def run_block(flags, pair, middle, other_pair, packed, bands, by_channel, beside=()):
    forcing = len(beside) > 0
    scratch = states(3 * SLAB)
    outs = [plane_shape(SLAB)]
    if forcing:
        scratch.append(pltpu.VMEM(plane_shape(SLAB), jnp.float32))
        outs = outs * 2
    kernel = functools.partial(block_kernel, by_channel, forcing)
    return call(kernel, outs, scratch, 4000000000, flags, pair, middle, other_pair, packed, bands, *beside)


def meet_kernel(flags, own, swapped, mine, near, rim, paid):
    lower = flags[0] == 0

    def even(a, b):
        return jnp.where(lower, own[a], swapped[b])

    for j in range(2):
        odd = jnp.where(lower, swapped[j], own[2 + j])
        near[j] = jnp.where(lower, swapped[2 + j], own[j])
        mine[j] = odd
        paid[3 + j] = odd
    for j in range(3):
        paid[j] = even(j, 1 + j)
    outer = even(0, 3)
    mine[2] = outer
    rim[0] = outer


def pay_kernel(flags, paid, far, home, out, both):
    lower = flags[0] == 0
    out[0] = jnp.where(lower, far[2], paid[0])
    out[1] = jnp.where(lower, paid[0], paid[1])
    out[2] = jnp.where(lower, paid[1], paid[2])
    out[3] = jnp.where(lower, paid[2], far[2])
    for j in range(2):
        out[4 + j] = paid[3 + j]
    for plane in range(6):
        both[plane] = out[plane]
    for plane in range(SLAB):
        both[6 + plane] = home[plane]


def sweep_kernel(first, final, step, flags, mine, near, far, paid, *refs):
    lower = flags[0] == 0
    if first:
        edge, *refs = refs
        forcing = [
            lambda: jnp.where(lower, edge[0], paid[0]),
            lambda: jnp.where(lower, paid[0], paid[1]),
            lambda: jnp.where(lower, paid[1], paid[2]),
            lambda: jnp.where(lower, paid[2], edge[0]),
            lambda: paid[3],
            lambda: paid[4],
        ]
    else:
        forcing = [functools.partial(lambda p: paid[p], p) for p in range(6)]
    packed, bands, pair, last, state, high, low = refs
    left_scale = jnp.where(lower, flags[1], 1).astype(jnp.float32)
    right_scale = jnp.where(lower, 1, flags[2]).astype(jnp.float32)
    for j in range(2):
        values = {
            j: jnp.where(lower, far[j], near[j]) * left_scale,
            2 + j: mine[j],
            4 + j: jnp.where(lower, near[j], far[j]) * right_scale,
        }
        for plane, value in values.items():
            state[plane] = value
            store_split(high, low, 0, plane, value)
    bias = offsets(packed.at[step])
    for at in (1, 3):
        outs = activations(high.at[0], low.at[0], bands[step], bias, at, 2)
        for plane, change in zip((at, at + 1), outs):
            value = state[plane] + COARSE * change + forcing[plane - 1]()
            if plane == 1:
                value = value * left_scale
            if plane == 4:
                value = value * right_scale
            state[plane] = value
            store_split(high, low, 1, plane, value)
            if plane in (2, 3):
                pair[plane - 2] = value
    outs = activations(high.at[1], low.at[1], bands[step + 1], offsets(packed.at[step + 1]), 2, 2)
    for j, change in enumerate(outs):
        value = state[2 + j] + COARSE * change + forcing[4 + j]()
        if final:
            even = pair[j]
            pair[j] = jnp.where(lower, even, value)
            last[j] = jnp.where(lower, value, even)
        else:
            pair[2 + j] = value
            last[j] = value


def run_sweep(first, final, step, flags, *arrays):
    kernel = functools.partial(sweep_kernel, first, final, step)
    outs = [plane_shape(2 if final else 4), plane_shape(2)]
    return call(kernel, outs, states(6), 900000000, flags, *arrays)


def finish_kernel(flags, kept, got, second, second_got, fourth, fourth_got, both, out):
    lower, chip = flags[0] == 0, flags[4]

    def early(pair, other, plane):
        j = plane % 2
        low = jnp.where(lower, pair[j], other[2 + j])
        return low if plane < 2 else jnp.where(lower, other[j], pair[2 + j])

    for plane in range(SLAB):
        j = plane % 2
        value = jnp.where(lower, kept[j], got[j]) if plane < 2 else jnp.where(lower, got[j], kept[j])
        value = jnp.where(chip == 1, early(second, second_got, plane), value)
        value = jnp.where(chip == 2, early(fourth, fourth_got, plane), value)
        value = jnp.where(chip == 0, both[6 + plane], value)
        out[0, :, plane] = value.reshape(out.shape[1], CELLS, LANES)


def residual_kernel(flags, beside, both, out):
    for plane in range(SLAB):
        value = both[6 + plane]
        value = jnp.where(flags[0] == 0, value, value - beside[plane])
        value = jnp.where(flags[5] == 0, 0.0, value)
        out[0, :, plane] = value.reshape(out.shape[1], CELLS, LANES)


def on_device(layers, slabs, initial, guess, weights, bias):
    layer = lax.axis_index("layer")
    slab = lax.axis_index("space")
    core = layer % 2
    lower = core == 0

    def send(array, target):
        pairs = []
        for l in range(layers):
            for s in range(slabs):
                to_l, to_s = target(l, s)
                pairs.append((l * slabs + s, (to_l % layers) * slabs + to_s % slabs))
        return lax.ppermute(array, ("layer", "space"), pairs)

    def paired(l, s):
        return l, s ^ 1

    def other_paired(l, s):
        to_s = s + 1 if s % 2 else s - 1
        return (l, to_s) if 0 <= to_s < slabs else (l ^ 1, s)

    def across(l, s):
        return l ^ 1, s

    def chips(flip, l):
        return 2 * (l // 2 ^ flip) + l % 2

    def zigzag(l, s, flip=0, end=1):
        to_s = s - 1 if l % 2 == 0 else s + 1
        if 0 <= to_s < slabs:
            return chips(flip, l ^ 1), to_s
        return chips(flip or end, l), s

    def zigzag_flipped(l, s):
        return zigzag(l, s, 3)

    def zigzag_on(l, s):
        return l ^ 1, (s - 1 if l % 2 == 0 else s + 1) % slabs

    def flipped(flip):
        return lambda l, s: (chips(flip, l), s)

    def shifted(by):
        return lambda l, s: (l + by, s)

    def far_chips(l, s):
        return (chips(2, l), s) if l // 2 in (1, 3) else (l ^ 1, s)

    flags = [core, slab > 0, slab < slabs - 1, layer < layers - 1, layer // 2, layer, layer == layers - 2, slab % 2]
    flags = jnp.stack(flags).astype(jnp.int32)
    group = weights.shape[0]

    start = jnp.where(layer == layers - 1, initial, guess[0])
    pair, other_pair = send(start, paired), send(start, other_paired)
    taps = jnp.pad(weights, ((0, 0), (0, 0), (0, BIAS_AT - weights.shape[2])))
    raw = jnp.concatenate([taps, jnp.broadcast_to(bias[:, :, None], bias.shape + (LANES,))], 2)
    raw_here = jnp.concatenate([send(raw, shifted(-1)), send(raw, shifted(-2))], 0)

    def pack(piece):
        count, channels, _ = piece.shape
        kernel = piece[:, :, : TAPS**3 * channels].reshape(count, channels, TAPS, TAPS, TAPS, channels)
        kernel = kernel.transpose(0, 3, 4, 1, 2, 5).reshape(count, KERNEL_ROWS, TAPS * channels)
        kernel = jnp.pad(kernel, ((0, 0), (0, 0), (0, LANES - TAPS * channels)))
        return jnp.concatenate([kernel, piece[:, :, BIAS_AT:]], 1)

    packed = pack(raw_here)
    bands = build(flags, packed[:group])
    coarse, _ = lax.optimization_barrier((raw[:1], packed))
    coarse_swapped = send(coarse, across)
    coarse = jnp.where(
        lower, jnp.concatenate([coarse, coarse_swapped], 0), jnp.concatenate([coarse_swapped, coarse], 0)
    )
    (relaxed,) = run_block(flags, pair, start, other_pair, packed[:group], bands, by_channel=True)

    pair, other_pair = send(relaxed, paired), send(relaxed, other_paired)
    beside = send(relaxed, across)
    sweep = pack(jnp.concatenate([send(coarse, flipped(2)), send(coarse, flipped(1)), coarse], 0))
    later, _ = lax.optimization_barrier((packed[group:], relaxed))
    bands = build(flags, later)
    pair, sweep = lax.optimization_barrier((pair, sweep))
    home, forced = run_block(flags, pair, relaxed, other_pair, later, bands, by_channel=False, beside=(beside,))

    swapped = send(forced, across)
    outs = [plane_shape(count) for count in (3, 2, 1, 5)]
    mine, near, rim, paid = call(meet_kernel, outs, [], 0, flags, forced, swapped)
    far, edge = send(mine, zigzag), send(rim, zigzag_flipped)
    sweep, _ = lax.optimization_barrier((sweep, near))
    bands = build(flags, sweep)
    paid_in = send(paid, shifted(-2))
    far, edge, bands = lax.optimization_barrier((far, edge, bands))
    pay, both = call(pay_kernel, [plane_shape(6), plane_shape(10)], [], 0, flags, paid, far, home)
    pay_two = send(pay, far_chips)
    second, last = run_sweep(True, False, 0, flags, mine, near, far, paid_in, edge, sweep, bands)

    near, far = send(last, across), send(last, zigzag_on)
    both, _ = lax.optimization_barrier((both, paid_in))
    both = send(both, shifted(2))
    fourth, last = run_sweep(False, False, 2, flags, last, near, far, pay_two, sweep, bands)

    second, _ = lax.optimization_barrier((second, far))
    second = send(second, far_chips)
    near, far = send(last, across), send(last, zigzag_on)
    fourth = send(fourth, shifted(-2))
    out = (1, initial.shape[0], SLAB, CELLS, LANES)
    kept, give = run_sweep(False, True, 4, flags, last, near, far, both, sweep, bands)

    second, fourth, give = lax.optimization_barrier((second, fourth, give))
    got, second_got, fourth_got = send(give, across), send(second, across), send(fourth, across)
    (residual,) = call(residual_kernel, [out], [], 0, flags, beside, both)
    (corrected,) = call(
        finish_kernel, [out], [], 0, flags, kept, got, second, second_got, fourth, fourth_got, both
    )
    return corrected, residual


def solution(mesh):
    layers, slabs = mesh.shape["layer"], mesh.shape["space"]
    in_specs = (
        P(None, "space", None, None),
        P("layer", None, "space", None, None),
        P("layer", None, None),
        P("layer", None),
    )
    out_specs = (P("layer", None, "space", None, None), P("layer", None, "space", None, None))
    return jax.shard_map(
        functools.partial(on_device, layers, slabs),
        mesh=mesh,
        in_specs=in_specs,
        out_specs=out_specs,
        check_vma=False,
    )
```

```python
import functools

import jax
import jax.numpy as jnp
from jax import lax
from jax.experimental import pallas as pl
from jax.experimental.pallas import tpu as pltpu
from jax.sharding import PartitionSpec as P

FINE = 0.25
COARSE = 1.0
LANES = 128
ROWS = 128
TAPS = 3
BAND = TAPS * ROWS
SLAB = 4
CELLS = 16
KERNEL_ROWS = 72
PACKED_ROWS = 80
BIAS_AT = 256
VMEM_LIMIT = 16 * 1024 * 1024


def split(value):
    high = value.astype(jnp.bfloat16)
    low = (value - high.astype(jnp.float32)).astype(jnp.bfloat16)
    return high, low


def build_kernel(flags, packed, out, taps):
    lane = lax.broadcasted_iota(jnp.int32, (LANES, BAND), 1)
    spread = jnp.where(lane // CELLS == lax.broadcasted_iota(jnp.int32, (LANES, BAND), 0), 1.0, 0.0)
    spread = spread.astype(jnp.bfloat16)
    row = lax.broadcasted_iota(jnp.int32, (CELLS, BAND), 0)
    offset = lax.broadcasted_iota(jnp.int32, (CELLS, BAND), 1) % CELLS - row
    blocks = BAND // CELLS
    for step in range(out.shape[0]):
        high, low = split(packed[step, :KERNEL_ROWS, :])
        both = jnp.concatenate([high, low], axis=0)
        taps[step] = jnp.dot(both, spread, preferred_element_type=jnp.float32)
        for part in range(2):
            for block in range(blocks):
                total = jnp.zeros((CELLS, BAND), jnp.float32)
                for tap in range(TAPS):
                    at = part * KERNEL_ROWS + tap * blocks + block
                    total = jnp.where(offset == tap - 1, taps[step, at : at + 1, :], total)
                total = total.astype(jnp.bfloat16)
                rows = slice(block * CELLS, (block + 1) * CELLS)
                out[step, rows, part * BAND : (part + 1) * BAND] = total
                if part == 0:
                    out[step, rows, 2 * BAND :] = total


def offsets(packed):
    rows = [jnp.broadcast_to(packed[at : at + 1, :], (CELLS, LANES)) for at in range(KERNEL_ROWS, PACKED_ROWS)]
    return jnp.concatenate(rows, axis=0)


def window(planes, at, count):
    pieces = [planes[(p - 1) * ROWS : (p + 2) * ROWS, :] for p in range(at, at + count)]
    return pieces[0] if count == 1 else jnp.concatenate(pieces, axis=1)


def activations(high, low, bands, bias, at, count):
    right = window(high, at, count)
    right = jnp.concatenate([right, right, window(low, at, count)], axis=0)
    mixed = jnp.dot(bands, right, preferred_element_type=jnp.float32)
    lane = lax.broadcasted_iota(jnp.int32, (ROWS, LANES), 1)
    results = []
    for j in range(count):
        part = mixed[:, j * LANES : (j + 1) * LANES]
        before = pltpu.roll(part[:ROWS], 1, axis=1)
        after = pltpu.roll(part[2 * ROWS :], LANES - 1, axis=1)
        conv = part[ROWS : 2 * ROWS] + bias
        conv = conv + jnp.where(lane == 0, 0.0, before) + jnp.where(lane == LANES - 1, 0.0, after)
        results.append(jnp.tanh(conv))
    return results


def store_split(high, low, slot, plane, value):
    h, l = split(value)
    high[slot, plane * ROWS : (plane + 1) * ROWS, :] = h
    low[slot, plane * ROWS : (plane + 1) * ROWS, :] = l


def block_kernel(by_channel, forcing, flags, pair, middle, other_pair, packed, bands, *refs):
    if forcing:
        beside, out, minus, state, high, low, coarse = refs
    else:
        out, state, high, low = refs
    planes = 3 * SLAB
    steps = bands.shape[0]
    scale = {0: flags[1].astype(jnp.float32), 2: flags[2].astype(jnp.float32)}

    def inside(plane, value):
        side = plane // SLAB
        return value * scale[side] if side != 1 else value

    def fetch(source, plane):
        return source[:, plane].reshape(ROWS, LANES) if by_channel else source[plane]

    paired_above = flags[7] == 0
    for plane in range(planes):
        side, at = plane // SLAB, plane % SLAB
        if side == 1:
            value = fetch(middle, at)
        else:
            above, below = (pair, other_pair) if side == 2 else (other_pair, pair)
            value = jnp.where(paired_above, fetch(above, at), fetch(below, at))
        value = inside(plane, value)
        state[plane] = value
        store_split(high, low, 0, plane, value)
    for step in range(steps):
        first, last = step + 1, planes - 1 - step
        now, later = step % 2, (step + 1) % 2
        bias = offsets(packed.at[step])
        for at in range(first, last, 2):
            outs = activations(high.at[now], low.at[now], bands[step], bias, at, 2)
            for plane, change in zip((at, at + 1), outs):
                old = state[plane]
                value = inside(plane, old + FINE * change)
                own = SLAB <= plane < 2 * SLAB
                if forcing and step == 0 and own:
                    coarse[plane - SLAB] = old + COARSE * change
                if step < steps - 1:
                    state[plane] = value
                    store_split(high, low, later, plane, value)
                else:
                    if not forcing:
                        out[plane - SLAB] = value
                        continue
                    at_home = plane - SLAB
                    minus[at_home] = value - coarse[at_home] * flags[3].astype(jnp.float32)
                    other = beside[at_home]
                    less = jnp.where(flags[6] == 1, other, value - other)
                    out[at_home] = jnp.where(flags[0] == 0, less, value)


VMEM = pl.BlockSpec(memory_space=pltpu.VMEM)
SMEM = pl.BlockSpec(memory_space=pltpu.SMEM)


def call(kernel, outs, scratch, flops, flags, *arrays):
    return pl.pallas_call(
        kernel,
        in_specs=[SMEM] + [VMEM] * len(arrays),
        out_specs=[VMEM] * len(outs),
        out_shape=[shape if hasattr(shape, "dtype") else jax.ShapeDtypeStruct(shape, jnp.float32) for shape in outs],
        scratch_shapes=scratch,
        compiler_params=pltpu.CompilerParams(vmem_limit_bytes=VMEM_LIMIT),
        cost_estimate=pl.CostEstimate(flops=flops, bytes_accessed=2000000, transcendentals=0),
    )(flags, *arrays)


def plane_shape(count):
    return (count, ROWS, LANES)


def build(flags, packed):
    steps = packed.shape[0]
    scratch = [pltpu.VMEM((steps, 2 * KERNEL_ROWS, BAND), jnp.float32)]
    shape = jax.ShapeDtypeStruct((steps, BAND, 3 * BAND), jnp.bfloat16)
    return call(build_kernel, [shape], scratch, steps * 20000000, flags, packed)[0]


def states(planes):
    return [
        pltpu.VMEM((planes, ROWS, LANES), jnp.float32),
        pltpu.VMEM((2, planes * ROWS, LANES), jnp.bfloat16),
        pltpu.VMEM((2, planes * ROWS, LANES), jnp.bfloat16),
    ]


def run_block(flags, pair, middle, other_pair, packed, bands, by_channel, beside=()):
    forcing = len(beside) > 0
    scratch = states(3 * SLAB)
    outs = [plane_shape(SLAB)]
    if forcing:
        scratch.append(pltpu.VMEM(plane_shape(SLAB), jnp.float32))
        outs = outs * 2
    kernel = functools.partial(block_kernel, by_channel, forcing)
    return call(kernel, outs, scratch, 4000000000, flags, pair, middle, other_pair, packed, bands, *beside)


def meet_kernel(flags, own, swapped, mine, near, rim, paid):
    lower = flags[0] == 0

    def even(a, b):
        return jnp.where(lower, own[a], swapped[b])

    for j in range(2):
        odd = jnp.where(lower, swapped[j], own[2 + j])
        near[j] = jnp.where(lower, swapped[2 + j], own[j])
        mine[j] = odd
        paid[3 + j] = odd
    for j in range(3):
        paid[j] = even(j, 1 + j)
    outer = even(0, 3)
    mine[2] = outer
    rim[0] = outer


def pay_kernel(flags, paid, far, home, out, both):
    lower = flags[0] == 0
    out[0] = jnp.where(lower, far[2], paid[0])
    out[1] = jnp.where(lower, paid[0], paid[1])
    out[2] = jnp.where(lower, paid[1], paid[2])
    out[3] = jnp.where(lower, paid[2], far[2])
    for j in range(2):
        out[4 + j] = paid[3 + j]
    for plane in range(6):
        both[plane] = out[plane]
    for plane in range(SLAB):
        both[6 + plane] = home[plane]


def sweep_kernel(first, final, step, flags, mine, near, far, paid, *refs):
    lower = flags[0] == 0
    if first:
        edge, *refs = refs
        forcing = [
            lambda: jnp.where(lower, edge[0], paid[0]),
            lambda: jnp.where(lower, paid[0], paid[1]),
            lambda: jnp.where(lower, paid[1], paid[2]),
            lambda: jnp.where(lower, paid[2], edge[0]),
            lambda: paid[3],
            lambda: paid[4],
        ]
    else:
        forcing = [functools.partial(lambda p: paid[p], p) for p in range(6)]
    packed, bands, pair, last, state, high, low = refs
    left_scale = jnp.where(lower, flags[1], 1).astype(jnp.float32)
    right_scale = jnp.where(lower, 1, flags[2]).astype(jnp.float32)
    for j in range(2):
        values = {
            j: jnp.where(lower, far[j], near[j]) * left_scale,
            2 + j: mine[j],
            4 + j: jnp.where(lower, near[j], far[j]) * right_scale,
        }
        for plane, value in values.items():
            state[plane] = value
            store_split(high, low, 0, plane, value)
    bias = offsets(packed.at[step])
    for at in (1, 3):
        outs = activations(high.at[0], low.at[0], bands[step], bias, at, 2)
        for plane, change in zip((at, at + 1), outs):
            value = state[plane] + COARSE * change + forcing[plane - 1]()
            if plane == 1:
                value = value * left_scale
            if plane == 4:
                value = value * right_scale
            state[plane] = value
            store_split(high, low, 1, plane, value)
            if plane in (2, 3):
                pair[plane - 2] = value
    outs = activations(high.at[1], low.at[1], bands[step + 1], offsets(packed.at[step + 1]), 2, 2)
    for j, change in enumerate(outs):
        value = state[2 + j] + COARSE * change + forcing[4 + j]()
        if final:
            even = pair[j]
            pair[j] = jnp.where(lower, even, value)
            last[j] = jnp.where(lower, value, even)
        else:
            pair[2 + j] = value
            last[j] = value


def run_sweep(first, final, step, flags, *arrays):
    kernel = functools.partial(sweep_kernel, first, final, step)
    outs = [plane_shape(2 if final else 4), plane_shape(2)]
    return call(kernel, outs, states(6), 900000000, flags, *arrays)


def finish_kernel(flags, kept, got, second, second_got, fourth, fourth_got, both, out):
    lower, chip = flags[0] == 0, flags[4]

    def early(pair, other, plane):
        j = plane % 2
        low = jnp.where(lower, pair[j], other[2 + j])
        return low if plane < 2 else jnp.where(lower, other[j], pair[2 + j])

    for plane in range(SLAB):
        j = plane % 2
        value = jnp.where(lower, kept[j], got[j]) if plane < 2 else jnp.where(lower, got[j], kept[j])
        value = jnp.where(chip == 1, early(second, second_got, plane), value)
        value = jnp.where(chip == 2, early(fourth, fourth_got, plane), value)
        value = jnp.where(chip == 0, both[6 + plane], value)
        out[0, :, plane] = value.reshape(out.shape[1], CELLS, LANES)


def residual_kernel(flags, beside, both, out):
    for plane in range(SLAB):
        value = both[6 + plane]
        value = jnp.where(flags[0] == 0, value, value - beside[plane])
        value = jnp.where(flags[5] == 0, 0.0, value)
        out[0, :, plane] = value.reshape(out.shape[1], CELLS, LANES)


def on_device(layers, slabs, initial, guess, weights, bias):
    layer = lax.axis_index("layer")
    slab = lax.axis_index("space")
    core = layer % 2
    lower = core == 0

    def send(array, target):
        pairs = []
        for l in range(layers):
            for s in range(slabs):
                to_l, to_s = target(l, s)
                pairs.append((l * slabs + s, (to_l % layers) * slabs + to_s % slabs))
        return lax.ppermute(array, ("layer", "space"), pairs)

    def paired(l, s):
        return l, s ^ 1

    def other_paired(l, s):
        to_s = s + 1 if s % 2 else s - 1
        return (l, to_s) if 0 <= to_s < slabs else (l ^ 1, s)

    def across(l, s):
        return l ^ 1, s

    def chips(flip, l):
        return 2 * (l // 2 ^ flip) + l % 2

    def zigzag(l, s, flip=0, end=1):
        to_s = s - 1 if l % 2 == 0 else s + 1
        if 0 <= to_s < slabs:
            return chips(flip, l ^ 1), to_s
        return chips(flip or end, l), s

    def zigzag_flipped(l, s):
        return zigzag(l, s, 3)

    def zigzag_on(l, s):
        return l ^ 1, (s - 1 if l % 2 == 0 else s + 1) % slabs

    def flipped(flip):
        return lambda l, s: (chips(flip, l), s)

    def shifted(by):
        return lambda l, s: (l + by, s)

    def far_chips(l, s):
        return (chips(2, l), s) if l // 2 in (1, 3) else (l ^ 1, s)

    flags = [core, slab > 0, slab < slabs - 1, layer < layers - 1, layer // 2, layer, layer == layers - 2, slab % 2]
    flags = jnp.stack(flags).astype(jnp.int32)
    group = weights.shape[0]

    start = jnp.where(layer == layers - 1, initial, guess[0])
    pair, other_pair = send(start, paired), send(start, other_paired)
    taps = jnp.pad(weights, ((0, 0), (0, 0), (0, BIAS_AT - weights.shape[2])))
    raw = jnp.concatenate([taps, jnp.broadcast_to(bias[:, :, None], bias.shape + (LANES,))], 2)
    raw_here = jnp.concatenate([send(raw, shifted(-1)), send(raw, shifted(-2))], 0)

    def pack(piece):
        count, channels, _ = piece.shape
        kernel = piece[:, :, : TAPS**3 * channels].reshape(count, channels, TAPS, TAPS, TAPS, channels)
        kernel = kernel.transpose(0, 3, 4, 1, 2, 5).reshape(count, KERNEL_ROWS, TAPS * channels)
        kernel = jnp.pad(kernel, ((0, 0), (0, 0), (0, LANES - TAPS * channels)))
        return jnp.concatenate([kernel, piece[:, :, BIAS_AT:]], 1)

    packed = pack(raw_here)
    bands = build(flags, packed[:group])
    coarse, _ = lax.optimization_barrier((raw[:1], packed))
    coarse_swapped = send(coarse, across)
    coarse = jnp.where(
        lower, jnp.concatenate([coarse, coarse_swapped], 0), jnp.concatenate([coarse_swapped, coarse], 0)
    )
    (relaxed,) = run_block(flags, pair, start, other_pair, packed[:group], bands, by_channel=True)

    pair, other_pair = send(relaxed, paired), send(relaxed, other_paired)
    beside = send(relaxed, across)
    sweep = pack(jnp.concatenate([send(coarse, flipped(2)), send(coarse, flipped(1)), coarse], 0))
    later, _ = lax.optimization_barrier((packed[group:], relaxed))
    bands = build(flags, later)
    pair, sweep = lax.optimization_barrier((pair, sweep))
    home, forced = run_block(flags, pair, relaxed, other_pair, later, bands, by_channel=False, beside=(beside,))

    swapped = send(forced, across)
    outs = [plane_shape(count) for count in (3, 2, 1, 5)]
    mine, near, rim, paid = call(meet_kernel, outs, [], 0, flags, forced, swapped)
    far, edge = send(mine, zigzag), send(rim, zigzag_flipped)
    sweep, _ = lax.optimization_barrier((sweep, near))
    bands = build(flags, sweep)
    paid_in = send(paid, shifted(-2))
    far, edge, bands = lax.optimization_barrier((far, edge, bands))
    pay, both = call(pay_kernel, [plane_shape(6), plane_shape(10)], [], 0, flags, paid, far, home)
    pay_two = send(pay, far_chips)
    paid_in, both = lax.optimization_barrier((paid_in, both))
    second, last = run_sweep(True, False, 0, flags, mine, near, far, paid_in, edge, sweep, bands)

    near, far = send(last, across), send(last, zigzag_on)
    both, _ = lax.optimization_barrier((both, last))
    both = send(both, shifted(2))
    fourth, last = run_sweep(False, False, 2, flags, last, near, far, pay_two, sweep, bands)

    second, _ = lax.optimization_barrier((second, far))
    second = send(second, far_chips)
    near, far = send(last, across), send(last, zigzag_on)
    fourth = send(fourth, shifted(-2))
    out = (1, initial.shape[0], SLAB, CELLS, LANES)
    second, far = lax.optimization_barrier((second, far))
    second_got = send(second, across)
    kept, give = run_sweep(False, True, 4, flags, last, near, far, both, sweep, bands)

    fourth, give = lax.optimization_barrier((fourth, give))
    got, fourth_got = send(give, across), send(fourth, across)
    (residual,) = call(residual_kernel, [out], [], 0, flags, beside, both)
    (corrected,) = call(
        finish_kernel, [out], [], 0, flags, kept, got, second, second_got, fourth, fourth_got, both
    )
    return corrected, residual


def solution(mesh):
    layers, slabs = mesh.shape["layer"], mesh.shape["space"]
    in_specs = (
        P(None, "space", None, None),
        P("layer", None, "space", None, None),
        P("layer", None, None),
        P("layer", None),
    )
    out_specs = (P("layer", None, "space", None, None), P("layer", None, "space", None, None))
    return jax.shard_map(
        functools.partial(on_device, layers, slabs),
        mesh=mesh,
        in_specs=in_specs,
        out_specs=out_specs,
        check_vma=False,
    )
```
